32 devices in a mesh: group: 2 (over y), expert: 4 (over x, core), dp: 4 (over z).
Axes of the slice: x: 2, y: 2, z: 4, core: 2. Of those that a mesh axis runs over, the one named last changes fastest.
Arguments:
- cotangent: bfloat16 [8192, 7168], P(('group', 'expert', 'dp')), parts along dimension 0, may hold values from -6 to 6
- expert_ids: int32 [8192, 8], P(('group', 'expert', 'dp')), parts along dimension 0, may hold values from 0 to 255, all different within a row; in each aligned block of 128 rows (0 to 127, 128 to 255, ...) at most 8 rows name the same one
- gate_values: float32 [8192, 8], P(('group', 'expert', 'dp')), parts along dimension 0, may hold values from 0.02 to 0.3
- hidden: bfloat16 [8, 4, 4, 2, 8, 1024], P(('group', 'expert'), 'dp'), parts along dimension 0, may hold values from -6 to 6
- down_weight: bfloat16 [4, 1024, 7168], P('expert', None, 'dp'), may hold values from -0.1875 to 0.1875
Outputs:
- fisher: float32 [8, 1024, 7168], P(('group', 'expert'), None, 'dp'), parts along dimension 0
- hidden_grad: bfloat16 [8, 4, 4, 2, 8, 1024], P(('group', 'expert'), 'dp'), parts along dimension 0
The draws below stay inside these ranges and needn't reach their ends.
There are 2 independent parts, one for each index of `group`. The reference program is written for one: setup_inputs(seed, part) draws one part's arguments, and reference() takes and returns one part's arrays. A program takes and returns all parts, laid end to end along the dimension named above; an argument that names none is the same for every part. Nothing has to cross between parts.
Inputs may be any that keep to these rules, and one draw needn't show every extreme that they name: `expert_ids`: each token names 8 different experts. In each aligned block of 128 tokens no expert is named by more than 8 tokens, a bound that some block reaches.
All inputs are finite; a program needn't handle non-finite values.
Results may differ from the reference program's by a relative error of at most 0.0051.
Values may be sent and summed in bfloat16 or wider, within the bound.
A program may use at most 128 MiB of HBM per device.

```python
import math
import jax
import jax.numpy as jnp
import numpy as np
from jax import lax

D = 7168
FF = 1024
ROUTED = 256
TOP = 8
GROUP = 128
CAP = 8
GROUPS_DEV = 2
EXPERTS_W = 4
TOKENS = 4096
N_EXPERT = 4
N_DP = 4


def level_of(own_key, extent, shards, least, top_value):
    gain = 1.0
    for position, blocks in shards:
        draws = jax.random.uniform(jax.random.fold_in(jax.random.fold_in(own_key, 6), position), (blocks,), jnp.float32, least / len(shards), top_value / len(shards))
        gain = gain * jnp.repeat(jnp.exp(draws), extent[position] // blocks).reshape((-1,) + (1,) * (len(extent) - 1 - position))
    return gain


def routed_block(key, own, number, rows, number_of, top, bound, skew):
    order = jax.random.permutation(key, number_of)
    packed, usual = load_shares(number_of, rows * top, bound, skew, True), load_shares(number_of, rows * top, bound, skew, False)
    places = jnp.arange(number_of)

    def named(lengths, offset_by):
        used = int((lengths > 0).sum())
        fixed = max(1, used // 4)
        passed = fixed + (places - fixed + offset_by * (used - fixed)) % max(1, number_of - fixed)
        return jnp.zeros((number_of,), jnp.int32).at[order[jnp.where(places < fixed, places, passed)]].set(jnp.asarray(lengths, jnp.int32))

    lengths = jnp.where(number % 4 == 0, named(packed, number // 4), named(usual, number - number // 4 - 1))
    mixed = jax.random.permutation(jax.random.fold_in(own, 3), number_of)
    source_of, taker = mixed[0:number_of // 2 * 2:2], mixed[1:number_of // 2 * 2:2]
    margin = jnp.minimum(lengths[source_of] - 1, bound - lengths[taker]) // 2
    margin = jnp.where((source_of == order[0]) | (taker == order[0]) | (lengths[taker] == 0), 0, jnp.maximum(margin, 0))
    passed = jax.random.randint(jax.random.fold_in(own, 4), (number_of // 2,), 0, 1 << 20) % (margin + 1)
    lengths = lengths.at[source_of].add(-passed).at[taker].add(passed)
    labels = jnp.searchsorted(jnp.cumsum(lengths), jnp.arange(rows * top), side="right").astype(jnp.int32)
    grid = labels.reshape(top, rows).T
    grid = grid[jax.random.permutation(jax.random.fold_in(own, 1), rows)]
    offset_by = jax.random.randint(jax.random.fold_in(own, 2), (rows, 1), 0, top)
    return jnp.take_along_axis(grid, (jnp.arange(top)[None, :] + offset_by) % top, axis=1)


def load_shares(number_of, total, most, slope, full):
    portions = [(1 << 20) // math.isqrt(rank ** slope) + 1 for rank in range(1, number_of + 1)]
    largest = most if full else min(most, max(-(-total // number_of), total * portions[0] // sum(portions)))
    least = 1 if total - largest >= number_of - 1 else 0
    counts, rest = [largest] + [least] * (number_of - 1), total - largest - least * (number_of - 1)
    while rest > 0:
        free = [i for i in range(1, number_of) if counts[i] < largest] or [i for i in range(1, number_of) if counts[i] < most]
        whole, left = sum([portions[i] for i in free]), rest
        for i in free:
            addition = min(most - counts[i], max(1, left * portions[i] // whole), rest)
            counts[i] = counts[i] + addition
            rest = rest - addition
    return np.array(counts)


def centred(key, shape, spread, most, shards=(), kind=jnp.bfloat16):
    values = jax.random.normal(key, shape, jnp.float32) * spread
    if len(shards) > 0:
        values = level_of(key, shape, shards, -0.22, 0.18) * values
    return jnp.clip(values, min=-most, max=most).astype(kind)


def setup_inputs(seed: int = 0, part: int = 0) -> dict:
    key_list = jax.random.split(jax.random.key(seed), 6)
    own_keys = jax.random.split(jax.random.fold_in(key_list[5], part), 6)
    cotangent = centred(own_keys[0], (TOKENS, D), 1.0, 6.0, ((0, 16),))
    expert_ids_keys = jax.random.split(jax.random.fold_in(own_keys[1], 1), TOKENS // GROUP)
    expert_ids_turns = jax.random.permutation(jax.random.fold_in(own_keys[1], 3), TOKENS // GROUP)
    expert_ids = jax.vmap(lambda own, number: routed_block(jax.random.fold_in(own_keys[1], 2), own, number, GROUP, ROUTED, TOP, CAP, 2))(expert_ids_keys, expert_ids_turns).reshape((TOKENS, TOP))
    gate_values = jnp.clip(0.02 + 0.28 * jax.random.uniform(own_keys[2], (TOKENS, TOP), jnp.float32) ** level_of(own_keys[2], (TOKENS, TOP), ((0, 16),), -0.2, 0.2), 0.02, 0.3)
    hidden = centred(own_keys[3], (EXPERTS_W, N_DP, N_EXPERT, GROUPS_DEV, CAP, FF), 1.0, 6.0, ((0, 4), (1, 4)))
    down_weight = centred(key_list[4], (EXPERTS_W, FF, D), FF ** -0.5, 0.1875, ((0, 4), (2, 4)))
    return {"cotangent": cotangent, "expert_ids": expert_ids, "gate_values": gate_values, "hidden": hidden, "down_weight": down_weight}


def reference(cotangent, expert_ids, gate_values, hidden, down_weight):
    experts = N_EXPERT
    ways = N_DP
    sources = experts * ways
    window = jnp.arange(experts, dtype=jnp.int32)
    match = expert_ids[:, :, None] == window[None, None, :]
    chosen = jnp.any(match, axis=1).astype(jnp.int32).reshape(sources, GROUPS_DEV, GROUP, experts)
    weight_sel = jnp.sum(jnp.where(match, gate_values[:, :, None], jnp.float32(0.0)), axis=1)
    weight_sel = weight_sel.reshape(sources, GROUPS_DEV, GROUP, experts)
    rank = jnp.cumsum(chosen, axis=2) - 1
    slots = jnp.arange(CAP, dtype=jnp.int32)
    place = (rank[..., None] == slots) & (chosen[..., None] == 1)
    token_id = jnp.arange(TOKENS, dtype=jnp.int32).reshape(sources, GROUPS_DEV, GROUP)
    slot_token = jnp.sum(jnp.where(place, token_id[:, :, :, None, None], 0), axis=2).astype(jnp.int32)
    slot_gate = jnp.sum(jnp.where(place, weight_sel[..., None], jnp.float32(0.0)), axis=2)
    slot_token = slot_token.reshape(experts, ways, GROUPS_DEV, experts, CAP).transpose(3, 1, 0, 2, 4)
    slot_gate = slot_gate.reshape(experts, ways, GROUPS_DEV, experts, CAP).transpose(3, 1, 0, 2, 4)

    def one_expert(items):
        tok_e, gate_e, hid_e, weight_e = items
        picked = cotangent[tok_e.reshape(-1)].astype(jnp.float32)
        routed = (picked * gate_e.reshape(-1)[:, None]).astype(jnp.bfloat16)
        grad = jnp.dot(routed, weight_e.T, preferred_element_type=jnp.float32).astype(jnp.bfloat16)
        grad = grad.reshape(hid_e.shape)
        blocks_c = routed.reshape(ways, experts, GROUPS_DEV, CAP, D).transpose(0, 2, 1, 3, 4)
        blocks_c = blocks_c.reshape(ways * GROUPS_DEV, experts * CAP, D)
        blocks_h = hid_e.transpose(0, 2, 1, 3, 4).reshape(ways * GROUPS_DEV, experts * CAP, FF)

        def add(total, pair):
            block_h, block_c = pair
            prod = jnp.dot(block_h.T, block_c, preferred_element_type=jnp.float32)
            return total + prod * prod, None

        total, unused = lax.scan(add, jnp.zeros((FF, D), jnp.float32), (blocks_h, blocks_c))
        return total * (1.0 / (ways * GROUPS_DEV)), grad

    fisher, hidden_grad = lax.map(one_expert, (slot_token, slot_gate, hidden, down_weight))
    return fisher, hidden_grad
```

```python
import functools

import jax
import jax.numpy as jnp
from jax import lax
from jax.experimental import pallas as pl
from jax.experimental.pallas import tpu as pltpu
from jax.sharding import PartitionSpec as P

GROUP = 128
MESH = pl.DeviceIdType.MESH


def partner(index, step, size):
    out, bit = 0, 1
    while bit < size:
        digit = (index // bit) % 2
        out = out + bit * ((1 - digit) if step & bit else digit)
        bit *= 2
    return out


def place_rows(ids, gates, experts, groups, cap):
    tokens, top = ids.shape
    slots = experts * groups * cap
    lanes = max(slots, 128)
    lane = lax.broadcasted_iota(jnp.int32, (tokens, lanes), 1)
    token = lax.broadcasted_iota(jnp.int32, (tokens, lanes), 0)
    lane_e = lax.div(lane, groups * cap)
    lane_j = lax.rem(lax.div(lane, cap), groups)
    lane_c = lax.rem(lane, cap).astype(jnp.float32)
    chosen = jnp.zeros((tokens, lanes), jnp.float32)
    gate = jnp.zeros((tokens, lanes), jnp.float32)
    for k in range(top):
        same = ids[:, k : k + 1] == lane_e
        chosen = chosen + jnp.where(same, 1.0, 0.0)
        gate = gate + jnp.where(same, gates[:, k : k + 1], 0.0)
    row = lax.broadcasted_iota(jnp.int32, (tokens, tokens), 0)
    col = lax.broadcasted_iota(jnp.int32, (tokens, tokens), 1)
    before = (col < row) & (lax.div(col, GROUP) == lax.div(row, GROUP))
    rank = jnp.dot(
        jnp.where(before, 1.0, 0.0).astype(jnp.bfloat16),
        chosen.astype(jnp.bfloat16),
        preferred_element_type=jnp.float32,
    )
    taken = (chosen > 0.5) & (rank == lane_c) & (lax.div(token, GROUP) == lane_j)
    place = jnp.where(taken, 1.0, 0.0)
    turned = place.T[:slots]
    slot_gate = jnp.sum(jnp.where(taken, gate, 0.0).T, axis=1, keepdims=True)[:slots]
    return turned.astype(jnp.bfloat16), slot_gate


def route_kernel(
    experts, ways, groups, cap,
    ids_ref, gates_ref, cot_hbm, hid_hbm, w_hbm,
    cols_hbm, hid_out, grad_ref,
    cot, w, routed, cols, hidden, part_out, part_in, own,
    cot_sem, w_sem, hid_sem, own_sem, out_sem,
    send_sem, recv_sem, hsend_sem, hrecv_sem, psend_sem, precv_sem,
):
    g, f, d = lax.axis_index("group"), lax.axis_index("expert"), lax.axis_index("dp")
    piece = groups * cap
    units = w.shape[0]
    width = w.shape[1]
    order = list(range(ways - 1, -1, -1))
    peers = [partner(d, k, ways) for k in range(ways)]

    def cot_copy(k):
        columns = pl.ds(pl.multiple_of(peers[k] * width, width), width)
        return pltpu.make_async_copy(cot_hbm.at[:, columns], cot.at[k], cot_sem.at[k])

    hid_copy = pltpu.make_async_copy(hid_hbm, hidden.at[d], hid_sem)
    w_copy = pltpu.make_async_copy(w_hbm, w, w_sem)
    hid_copy.start()
    for k in order:
        cot_copy(k).start()
    w_copy.start()

    barrier = pltpu.get_barrier_semaphore()
    total = experts * ways

    def greet(i, carry):
        other = (f * ways + d + i) % total
        pl.semaphore_signal(
            barrier, inc=1, device_id=(g, other // ways, other % ways), device_id_type=MESH
        )
        return carry

    lax.fori_loop(1, total, greet, 0)
    place, slot_gate = place_rows(ids_ref[...], gates_ref[...], experts, groups, cap)
    pl.semaphore_wait(barrier, total - 1)

    def hid_send(k):
        return pltpu.make_async_remote_copy(
            src_ref=hidden.at[d], dst_ref=hidden.at[d],
            send_sem=hsend_sem.at[k], recv_sem=hrecv_sem.at[k],
            device_id=(g, f, peers[k]), device_id_type=MESH,
        )

    def row_send(k, i):
        e = (f + i) % experts
        rows = pl.ds(pl.multiple_of(e * piece, piece), piece)
        mine = pl.ds(pl.multiple_of(f * piece, piece), piece)
        return pltpu.make_async_remote_copy(
            src_ref=routed.at[k, rows], dst_ref=cols.at[d, mine],
            send_sem=send_sem.at[k, i], recv_sem=recv_sem.at[k, i],
            device_id=(g, e, peers[k]), device_id_type=MESH,
        )

    def row_wait(k, i):
        source = (f + experts - i) % experts
        rows = pl.ds(pl.multiple_of(source * piece, piece), piece)
        return pltpu.make_async_remote_copy(
            src_ref=routed.at[k, rows], dst_ref=cols.at[peers[k], rows],
            send_sem=send_sem.at[k, i], recv_sem=recv_sem.at[k, i],
            device_id=(g, source, peers[k]), device_id_type=MESH,
        )

    hid_copy.wait()
    for k in order:
        if k:
            hid_send(k).start()

    chunk = 256 if width % 256 == 0 else 128
    mine = pl.ds(pl.multiple_of(f * piece, piece), piece)
    own_copy = pltpu.make_async_copy(routed.at[0, mine], cols.at[d, mine], own_sem)
    for k in order:
        cot_copy(k).wait()

        @pl.loop(0, width // chunk)
        def pick(n):
            at = pl.ds(pl.multiple_of(n * chunk, chunk), chunk)
            picked = jnp.dot(place, cot[k, :, at], preferred_element_type=jnp.float32)
            routed[k, :, at] = (picked * slot_gate).astype(jnp.bfloat16)

        for i in range(experts):
            if k or i:
                row_send(k, i).start()
            else:
                own_copy.start()

    w_copy.wait()
    tile = 256

    def part_send(k):
        return pltpu.make_async_remote_copy(
            src_ref=part_out.at[k], dst_ref=part_in.at[k],
            send_sem=psend_sem.at[k], recv_sem=precv_sem.at[k],
            device_id=(g, f, peers[k]), device_id_type=MESH,
        )

    def cols_out(k):
        return pltpu.make_async_copy(cols.at[peers[k]], cols_hbm.at[peers[k]], out_sem.at[0, k])

    def hid_back(k):
        return pltpu.make_async_copy(hidden.at[peers[k]], hid_out.at[peers[k]], out_sem.at[1, k])

    def hid_wait(k):
        return pltpu.make_async_remote_copy(
            src_ref=hidden.at[peers[k]], dst_ref=hidden.at[peers[k]],
            send_sem=hsend_sem.at[k], recv_sem=hrecv_sem.at[k],
            device_id=(g, f, peers[k]), device_id_type=MESH,
        )

    for k in order:
        for i in range(experts):
            if k or i:
                row_wait(k, i).wait_recv()
            else:
                own_copy.wait()
        cols_out(k).start()

        @pl.loop(0, units // tile)
        def multiply(n):
            at = pl.ds(pl.multiple_of(n * tile, tile), tile)
            part = lax.dot_general(
                cols[peers[k]], w[at, :], (((1,), (1,)), ((), ())),
                preferred_element_type=jnp.float32,
            )
            if k:
                part_out[k, :, at] = part.astype(jnp.bfloat16)
            else:
                own[:, at] = part

        if k:
            part_send(k).start()

    for k in order:
        if k:
            hid_wait(k).wait_recv()
        hid_back(k).start()
    acc = own[...]
    for k in order:
        if k:
            part_send(k).wait_recv()
            acc = acc + part_in[k].astype(jnp.float32)
    grad_ref[...] = acc.astype(jnp.bfloat16)
    for k in order:
        cols_out(k).wait()
        hid_back(k).wait()
        for i in range(experts):
            if k or i:
                row_send(k, i).wait_send()
        if k:
            hid_send(k).wait_send()
            part_send(k).wait_send()


def fisher_kernel(groups, cap, scale, cols_ref, hid_ref, out_ref):
    ways, rows, width = cols_ref.shape
    tile = out_ref.shape[0]
    lane = lax.broadcasted_iota(jnp.int32, (tile, rows), 1)
    lane_j = lax.rem(lax.div(lane, cap), groups)
    turned = [hid_ref[s].astype(jnp.float32).T for s in range(ways)]
    lhs = [
        [jnp.where(lane_j == j, turned[s], 0.0).astype(jnp.bfloat16) for j in range(groups)]
        for s in range(ways)
    ]
    chunk = 256 if width % 256 == 0 else 128
    for n in range(width // chunk):
        at = slice(n * chunk, (n + 1) * chunk)
        acc = jnp.zeros((tile, chunk), jnp.float32)
        for s in range(ways):
            for j in range(groups):
                prod = jnp.dot(lhs[s][j], cols_ref[s, :, at], preferred_element_type=jnp.float32)
                acc = acc + prod * prod
        out_ref[:, at] = acc * scale


def per_device(cotangent, expert_ids, gate_values, hidden, down_weight):
    experts = lax.axis_size("expert")
    ways = lax.axis_size("dp")
    groups, cap, units = hidden.shape[3], hidden.shape[4], hidden.shape[5]
    piece = groups * cap
    slots = experts * piece
    width = down_weight.shape[2]
    tokens = cotangent.shape[0]
    any_spec = pl.BlockSpec(memory_space=pl.ANY)
    vmem_spec = pl.BlockSpec(memory_space=pltpu.VMEM)
    bf16 = jnp.bfloat16
    columns, gathered, grad = pl.pallas_call(
        functools.partial(route_kernel, experts, ways, groups, cap),
        out_shape=(
            jax.ShapeDtypeStruct((ways, slots, width), bf16),
            jax.ShapeDtypeStruct((ways, slots, units), bf16),
            jax.ShapeDtypeStruct((slots, units), bf16),
        ),
        in_specs=[vmem_spec, vmem_spec, any_spec, any_spec, any_spec],
        out_specs=(any_spec, any_spec, vmem_spec),
        scratch_shapes=[
            pltpu.VMEM((ways, tokens, width), bf16),
            pltpu.VMEM((units, width), bf16),
            pltpu.VMEM((ways, slots, width), bf16),
            pltpu.VMEM((ways, slots, width), bf16),
            pltpu.VMEM((ways, slots, units), bf16),
            pltpu.VMEM((ways, slots, units), bf16),
            pltpu.VMEM((ways, slots, units), bf16),
            pltpu.VMEM((slots, units), jnp.float32),
            pltpu.SemaphoreType.DMA((ways,)),
            pltpu.SemaphoreType.DMA,
            pltpu.SemaphoreType.DMA,
            pltpu.SemaphoreType.DMA,
            pltpu.SemaphoreType.DMA((2, ways)),
            pltpu.SemaphoreType.DMA((ways, experts)),
            pltpu.SemaphoreType.DMA((ways, experts)),
            pltpu.SemaphoreType.DMA((ways,)),
            pltpu.SemaphoreType.DMA((ways,)),
            pltpu.SemaphoreType.DMA((ways,)),
            pltpu.SemaphoreType.DMA((ways,)),
        ],
        compiler_params=pltpu.CompilerParams(
            collective_id=0, has_side_effects=True, vmem_limit_bytes=48 * 2**20
        ),
        name="route",
    )(expert_ids, gate_values, cotangent, hidden.reshape(slots, units), down_weight[0])
    tile = 128
    fisher = pl.pallas_call(
        functools.partial(fisher_kernel, groups, cap, 1.0 / (ways * groups)),
        out_shape=jax.ShapeDtypeStruct((units, width), jnp.float32),
        grid=(units // tile,),
        in_specs=[
            pl.BlockSpec((ways, slots, width), lambda i: (0, 0, 0)),
            pl.BlockSpec((ways, slots, tile), lambda i: (0, 0, i)),
        ],
        out_specs=pl.BlockSpec((tile, width), lambda i: (i, 0)),
        compiler_params=pltpu.CompilerParams(vmem_limit_bytes=32 * 2**20),
        name="fisher",
    )(columns, gathered)
    return (fisher[None], grad.reshape(hidden.shape))


def solution(mesh):
    in_specs = (
        P(("group", "expert", "dp"), None),
        P(("group", "expert", "dp"), None),
        P(("group", "expert", "dp"), None),
        P(("group", "expert"), "dp", None, None, None, None),
        P("expert", None, "dp"),
    )
    out_specs = (
        P(("group", "expert"), None, "dp"),
        P(("group", "expert"), "dp", None, None, None, None),
    )
    return jax.shard_map(
        per_device, mesh=mesh, in_specs=in_specs, out_specs=out_specs, check_vma=False
    )
```

```python
import functools

import jax
import jax.numpy as jnp
from jax import lax
from jax.experimental import pallas as pl
from jax.experimental.pallas import tpu as pltpu
from jax.sharding import PartitionSpec as P

GROUP = 128
MESH = pl.DeviceIdType.MESH


def partner(index, step, size):
    out, bit = 0, 1
    while bit < size:
        digit = (index // bit) % 2
        out = out + bit * ((1 - digit) if step & bit else digit)
        bit *= 2
    return out


def place_rows(ids, gates, experts, groups, cap):
    top, tokens = ids.shape
    slots = experts * groups * cap
    slot = lax.broadcasted_iota(jnp.int32, (slots, tokens), 0)
    token = lax.broadcasted_iota(jnp.int32, (slots, tokens), 1)
    slot_e = lax.div(slot, groups * cap)
    slot_j = lax.rem(lax.div(slot, cap), groups)
    slot_c = lax.rem(slot, cap).astype(jnp.float32)
    chosen = jnp.zeros((slots, tokens), jnp.float32)
    gate = jnp.zeros((slots, tokens), jnp.float32)
    for k in range(top):
        same = ids[k : k + 1, :] == slot_e
        chosen = chosen + jnp.where(same, 1.0, 0.0)
        gate = gate + jnp.where(same, gates[k : k + 1, :], 0.0)
    row = lax.broadcasted_iota(jnp.int32, (tokens, tokens), 0)
    col = lax.broadcasted_iota(jnp.int32, (tokens, tokens), 1)
    before = (row < col) & (lax.div(col, GROUP) == lax.div(row, GROUP))
    rank = jnp.dot(
        chosen.astype(jnp.bfloat16),
        jnp.where(before, 1.0, 0.0).astype(jnp.bfloat16),
        preferred_element_type=jnp.float32,
    )
    taken = (chosen > 0.5) & (rank == slot_c) & (lax.div(token, GROUP) == slot_j)
    slot_gate = jnp.sum(jnp.where(taken, gate, 0.0), axis=1, keepdims=True)
    return jnp.where(taken, 1.0, 0.0).astype(jnp.bfloat16), slot_gate


def lowest(k):
    return k & -k


def route_kernel(
    experts, ways, groups, cap,
    ids_hbm, gates_hbm, cot_hbm, hid_hbm, w_hbm,
    fisher_ref, grad_ref,
    ids, gates, cot, w, routed, cols, hidden, part_out, part_in, acc, turned,
    small_sem, cot_sem, w_sem, hid_sem, own_sem,
    send_sem, recv_sem, hsend_sem, hrecv_sem, psend_sem, precv_sem,
):
    g, f, d = lax.axis_index("group"), lax.axis_index("expert"), lax.axis_index("dp")
    piece = groups * cap
    units, width = w.shape
    slots = experts * piece
    order = list(range(ways - 1, -1, -1))
    peers = [partner(d, k, ways) for k in range(ways)]

    def cot_copy(k):
        columns = pl.ds(pl.multiple_of(peers[k] * width, width), width)
        return pltpu.make_async_copy(cot_hbm.at[:, columns], cot.at[k], cot_sem.at[k])

    ids_copy = pltpu.make_async_copy(ids_hbm, ids, small_sem.at[0])
    gates_copy = pltpu.make_async_copy(gates_hbm, gates, small_sem.at[1])
    hid_copy = pltpu.make_async_copy(hid_hbm, hidden.at[0], hid_sem)
    w_copy = pltpu.make_async_copy(w_hbm, w, w_sem)
    ids_copy.start()
    gates_copy.start()
    hid_copy.start()
    for k in order:
        cot_copy(k).start()
    w_copy.start()

    barrier = pltpu.get_barrier_semaphore()
    total = experts * ways

    def greet(i, carry):
        other = (f * ways + d + i) % total
        pl.semaphore_signal(
            barrier, inc=1, device_id=(g, other // ways, other % ways), device_id_type=MESH
        )
        return carry

    lax.fori_loop(1, total, greet, 0)
    ids_copy.wait()
    gates_copy.wait()
    place, slot_gate = place_rows(ids[...], gates[...], experts, groups, cap)
    hid_copy.wait()
    pl.semaphore_wait(barrier, total - 1)

    def hid_send(k):
        return pltpu.make_async_remote_copy(
            src_ref=hidden.at[k - lowest(k)], dst_ref=hidden.at[k],
            send_sem=hsend_sem.at[k], recv_sem=hrecv_sem.at[k],
            device_id=(g, f, peers[lowest(k)]), device_id_type=MESH,
        )

    def part_send(k):
        return pltpu.make_async_remote_copy(
            src_ref=part_out.at[k], dst_ref=part_in.at[k],
            send_sem=psend_sem.at[k], recv_sem=precv_sem.at[k],
            device_id=(g, f, peers[lowest(k)]), device_id_type=MESH,
        )

    def row_send(k, i):
        e = (f + i) % experts
        rows = pl.ds(pl.multiple_of(e * piece, piece), piece)
        mine = pl.ds(pl.multiple_of(f * piece, piece), piece)
        return pltpu.make_async_remote_copy(
            src_ref=routed.at[k, rows], dst_ref=cols.at[k, mine],
            send_sem=send_sem.at[k, i], recv_sem=recv_sem.at[k, i],
            device_id=(g, e, peers[k]), device_id_type=MESH,
        )

    def row_wait(k, i):
        source = (f + experts - i) % experts
        rows = pl.ds(pl.multiple_of(source * piece, piece), piece)
        return pltpu.make_async_remote_copy(
            src_ref=routed.at[k, rows], dst_ref=cols.at[k, rows],
            send_sem=send_sem.at[k, i], recv_sem=recv_sem.at[k, i],
            device_id=(g, source, peers[k]), device_id_type=MESH,
        )

    gather = sorted(range(1, ways), key=lambda k: -lowest(k))
    for k in gather:
        if k == lowest(k):
            hid_send(k).start()

    chunk = 256 if width % 256 == 0 else 128
    mine = pl.ds(pl.multiple_of(f * piece, piece), piece)
    own_copy = pltpu.make_async_copy(routed.at[0, mine], cols.at[0, mine], own_sem)
    for k in order:
        cot_copy(k).wait()
        for n in range(width // chunk):
            at = slice(n * chunk, (n + 1) * chunk)
            picked = jnp.dot(place, cot[k, :, at], preferred_element_type=jnp.float32)
            routed[k, :, at] = (picked * slot_gate).astype(jnp.bfloat16)
        for i in range(experts):
            if k or i:
                row_send(k, i).start()
            else:
                own_copy.start()

    arrived = set()

    def hid_arrive(k):
        if k and k not in arrived:
            hid_send(k).wait_recv()
            arrived.add(k)

    for k in gather:
        if k != lowest(k):
            hid_arrive(k - lowest(k))
            hid_send(k).start()

    w_copy.wait()
    tile = 256
    lane = lax.broadcasted_iota(jnp.int32, (units, 2 * slots), 1)
    lane_j = lax.rem(lax.div(lane, cap), groups)
    lane_half = lax.div(lane, slots)
    scale = 1.0 / (ways * groups)

    def combine(k):
        part_send(k).wait_recv()
        acc[k - lowest(k)] += part_in[k].astype(jnp.float32)

    def send_part(k):
        part_out[k] = acc[k].astype(jnp.bfloat16)
        part_send(k).start()

    for first in range(0, ways, 2):
        for k in (first + 1, first):
            for i in range(experts):
                if k or i:
                    row_wait(k, i).wait_recv()
                else:
                    own_copy.wait()

        pair = cols[first : first + 2].reshape(2 * slots, width)
        for n in range(units // tile):
            at = slice(n * tile, (n + 1) * tile)
            part = lax.dot_general(
                pair, w[at, :], (((1,), (1,)), ((), ())), preferred_element_type=jnp.float32
            )
            acc[first, :, at] = part[:slots]
            part_out[first + 1, :, at] = part[slots:].astype(jnp.bfloat16)
        part_send(first + 1).start()

        if first + 2 == ways:
            for k in range(ways - 2, 0, -2):
                combine(k + 1)
                if lowest(k) == 2:
                    send_part(k)

        hid_arrive(first + 1)
        hid_arrive(first)
        flat = hidden[first : first + 2].reshape(2 * slots, units).astype(jnp.float32).T
        for h in range(2):
            for j in range(groups):
                keep = (lane_half == h) & (lane_j == j)
                turned[h * groups + j] = jnp.where(keep, flat, 0.0).astype(jnp.bfloat16)

        @pl.loop(0, width // chunk)
        def squares(n):
            at = pl.ds(pl.multiple_of(n * chunk, chunk), chunk)
            block = cols[first : first + 2, :, at].reshape(2 * slots, chunk)
            step = 128
            for m in range(units // step):
                rows = slice(m * step, (m + 1) * step)
                total_sq = None
                for b in range(2 * groups):
                    prod = jnp.dot(turned[b, rows, :], block, preferred_element_type=jnp.float32)
                    total_sq = prod * prod if total_sq is None else total_sq + prod * prod
                if first:
                    total_sq = total_sq + fisher_ref[rows, at]
                if first + 2 == ways:
                    total_sq = total_sq * scale
                fisher_ref[rows, at] = total_sq

    combine(1)
    bit = 2
    while bit < ways:
        for k in range(2 * bit, ways, 2 * bit):
            combine(k + bit)
            if lowest(k) == 2 * bit:
                send_part(k)
        combine(bit)
        bit *= 2
    grad_ref[...] = acc[0].astype(jnp.bfloat16)
    for k in order:
        for i in range(experts):
            if k or i:
                row_send(k, i).wait_send()
        if k:
            hid_send(k).wait_send()
            part_send(k).wait_send()


def per_device(cotangent, expert_ids, gate_values, hidden, down_weight):
    experts = lax.axis_size("expert")
    ways = lax.axis_size("dp")
    groups, cap, units = hidden.shape[3], hidden.shape[4], hidden.shape[5]
    piece = groups * cap
    slots = experts * piece
    width = down_weight.shape[2]
    tokens, top = expert_ids.shape
    hbm_spec = pl.BlockSpec(memory_space=pltpu.HBM)
    vmem_spec = pl.BlockSpec(memory_space=pltpu.VMEM)
    bf16 = jnp.bfloat16
    operands = (
        expert_ids.T, gate_values.T, cotangent, hidden.reshape(slots, units), down_weight[0],
    )
    fisher, grad = pl.pallas_call(
        functools.partial(route_kernel, experts, ways, groups, cap),
        out_shape=(
            pltpu.VMEM((units, width), jnp.float32),
            pltpu.VMEM((slots, units), bf16),
        ),
        in_specs=[hbm_spec] * 5,
        out_specs=(vmem_spec, vmem_spec),
        scratch_shapes=[
            pltpu.VMEM((top, tokens), jnp.int32),
            pltpu.VMEM((top, tokens), jnp.float32),
            pltpu.VMEM((ways, tokens, width), bf16),
            pltpu.VMEM((units, width), bf16),
            pltpu.VMEM((ways, slots, width), bf16),
            pltpu.VMEM((ways, slots, width), bf16),
            pltpu.VMEM((ways, slots, units), bf16),
            pltpu.VMEM((ways, slots, units), bf16),
            pltpu.VMEM((ways, slots, units), bf16),
            pltpu.VMEM((ways, slots, units), jnp.float32),
            pltpu.VMEM((2 * groups, units, 2 * slots), bf16),
            pltpu.SemaphoreType.DMA((2,)),
            pltpu.SemaphoreType.DMA((ways,)),
            pltpu.SemaphoreType.DMA,
            pltpu.SemaphoreType.DMA,
            pltpu.SemaphoreType.DMA,
            pltpu.SemaphoreType.DMA((ways, experts)),
            pltpu.SemaphoreType.DMA((ways, experts)),
            pltpu.SemaphoreType.DMA((ways,)),
            pltpu.SemaphoreType.DMA((ways,)),
            pltpu.SemaphoreType.DMA((ways,)),
            pltpu.SemaphoreType.DMA((ways,)),
        ],
        compiler_params=pltpu.CompilerParams(
            collective_id=0, has_side_effects=True, vmem_limit_bytes=50 * 2**20
        ),
        name="route",
    )(*(pltpu.with_memory_space_constraint(x, pltpu.HBM) for x in operands))
    return (fisher[None], grad.reshape(hidden.shape))


def solution(mesh):
    in_specs = (
        P(("group", "expert", "dp"), None),
        P(("group", "expert", "dp"), None),
        P(("group", "expert", "dp"), None),
        P(("group", "expert"), "dp", None, None, None, None),
        P("expert", None, "dp"),
    )
    out_specs = (
        P(("group", "expert"), None, "dp"),
        P(("group", "expert"), "dp", None, None, None, None),
    )
    return jax.shard_map(
        per_device, mesh=mesh, in_specs=in_specs, out_specs=out_specs, check_vma=False
    )
```

```python
import functools

import jax
import jax.numpy as jnp
from jax import lax
from jax.experimental import pallas as pl
from jax.experimental.pallas import tpu as pltpu
from jax.sharding import PartitionSpec as P

GROUP = 128
MESH = pl.DeviceIdType.MESH


def partner(index, step, size):
    out, bit = 0, 1
    while bit < size:
        digit = (index // bit) % 2
        out = out + bit * ((1 - digit) if step & bit else digit)
        bit *= 2
    return out


def place_rows(ids, gates, experts, groups, cap):
    top, tokens = ids.shape
    slots = experts * groups * cap
    slot = lax.broadcasted_iota(jnp.int32, (slots, tokens), 0)
    token = lax.broadcasted_iota(jnp.int32, (slots, tokens), 1)
    slot_e = lax.div(slot, groups * cap)
    slot_j = lax.rem(lax.div(slot, cap), groups)
    slot_c = lax.rem(slot, cap).astype(jnp.float32)
    chosen = jnp.zeros((slots, tokens), jnp.float32)
    gate = jnp.zeros((slots, tokens), jnp.float32)
    for k in range(top):
        same = ids[k : k + 1, :] == slot_e
        chosen = chosen + jnp.where(same, 1.0, 0.0)
        gate = gate + jnp.where(same, gates[k : k + 1, :], 0.0)
    row = lax.broadcasted_iota(jnp.int32, (tokens, tokens), 0)
    col = lax.broadcasted_iota(jnp.int32, (tokens, tokens), 1)
    before = (row < col) & (lax.div(col, GROUP) == lax.div(row, GROUP))
    rank = jnp.dot(
        chosen.astype(jnp.bfloat16),
        jnp.where(before, 1.0, 0.0).astype(jnp.bfloat16),
        preferred_element_type=jnp.float32,
    )
    taken = (chosen > 0.5) & (rank == slot_c) & (lax.div(token, GROUP) == slot_j)
    slot_gate = jnp.sum(jnp.where(taken, gate, 0.0), axis=1, keepdims=True)
    return jnp.where(taken, 1.0, 0.0).astype(jnp.bfloat16), slot_gate


def lowest(k):
    return k & -k


def route_kernel(
    experts, ways, groups, cap,
    ids_hbm, gates_hbm, cot_hbm, hid_hbm, w_hbm,
    fisher_ref, grad_ref,
    ids, gates, cot, w, routed, cols, hidden, part_out, part_in, acc, turned,
    small_sem, cot_sem, w_sem, hid_sem, own_sem,
    send_sem, recv_sem, hsend_sem, hrecv_sem, psend_sem, precv_sem,
):
    g, f, d = lax.axis_index("group"), lax.axis_index("expert"), lax.axis_index("dp")
    piece = groups * cap
    units, width = w.shape
    slots = experts * piece
    order = list(range(ways - 1, 1, -2)) + [1, 0] + list(range(ways - 2, 1, -2))
    peers = [partner(d, k, ways) for k in range(ways)]

    def cot_copy(k):
        columns = pl.ds(pl.multiple_of(peers[k] * width, width), width)
        return pltpu.make_async_copy(cot_hbm.at[:, columns], cot.at[k], cot_sem.at[k])

    ids_copy = pltpu.make_async_copy(ids_hbm, ids, small_sem.at[0])
    gates_copy = pltpu.make_async_copy(gates_hbm, gates, small_sem.at[1])
    hid_copy = pltpu.make_async_copy(hid_hbm, hidden.at[0], hid_sem)
    w_copy = pltpu.make_async_copy(w_hbm, w, w_sem)
    ids_copy.start()
    gates_copy.start()
    hid_copy.start()
    for k in order:
        cot_copy(k).start()
    w_copy.start()

    barrier = pltpu.get_barrier_semaphore()
    total = experts * ways

    def greet(i, carry):
        other = (f * ways + d + i) % total
        pl.semaphore_signal(
            barrier, inc=1, device_id=(g, other // ways, other % ways), device_id_type=MESH
        )
        return carry

    lax.fori_loop(1, total, greet, 0)
    ids_copy.wait()
    gates_copy.wait()
    place, slot_gate = place_rows(ids[...], gates[...], experts, groups, cap)
    hid_copy.wait()
    pl.semaphore_wait(barrier, total - 1)

    def hid_send(k):
        return pltpu.make_async_remote_copy(
            src_ref=hidden.at[k - lowest(k)], dst_ref=hidden.at[k],
            send_sem=hsend_sem.at[k], recv_sem=hrecv_sem.at[k],
            device_id=(g, f, peers[lowest(k)]), device_id_type=MESH,
        )

    parts = 2
    span = units // parts

    def part_send(k, h):
        at = pl.ds(h * span, span)
        return pltpu.make_async_remote_copy(
            src_ref=part_out.at[k, :, at], dst_ref=part_in.at[k, :, at],
            send_sem=psend_sem.at[k, h], recv_sem=precv_sem.at[k, h],
            device_id=(g, f, peers[lowest(k)]), device_id_type=MESH,
        )

    def row_send(k, i):
        e = (f + i) % experts
        rows = pl.ds(pl.multiple_of(e * piece, piece), piece)
        mine = pl.ds(pl.multiple_of(f * piece, piece), piece)
        return pltpu.make_async_remote_copy(
            src_ref=routed.at[k, rows], dst_ref=cols.at[k, mine],
            send_sem=send_sem.at[k, i], recv_sem=recv_sem.at[k, i],
            device_id=(g, e, peers[k]), device_id_type=MESH,
        )

    def row_wait(k, i):
        source = (f + experts - i) % experts
        rows = pl.ds(pl.multiple_of(source * piece, piece), piece)
        return pltpu.make_async_remote_copy(
            src_ref=routed.at[k, rows], dst_ref=cols.at[k, rows],
            send_sem=send_sem.at[k, i], recv_sem=recv_sem.at[k, i],
            device_id=(g, source, peers[k]), device_id_type=MESH,
        )

    gather = sorted(range(1, ways), key=lambda k: -lowest(k))
    for k in gather:
        if k == lowest(k):
            hid_send(k).start()

    chunk = 256 if width % 256 == 0 else 128
    mine = pl.ds(pl.multiple_of(f * piece, piece), piece)
    own_copy = pltpu.make_async_copy(routed.at[0, mine], cols.at[0, mine], own_sem)
    for k in order:
        cot_copy(k).wait()
        for n in range(width // chunk):
            at = slice(n * chunk, (n + 1) * chunk)
            picked = jnp.dot(place, cot[k, :, at], preferred_element_type=jnp.float32)
            routed[k, :, at] = (picked * slot_gate).astype(jnp.bfloat16)
        for i in range(experts):
            if k or i:
                row_send(k, i).start()
            else:
                own_copy.start()

    arrived = set()

    def hid_arrive(k):
        if k and k not in arrived:
            hid_send(k).wait_recv()
            arrived.add(k)

    for k in gather:
        if k != lowest(k):
            hid_arrive(k - lowest(k))
            hid_send(k).start()

    w_copy.wait()
    tile = 256
    lane = lax.broadcasted_iota(jnp.int32, (units, 2 * slots), 1)
    lane_j = lax.rem(lax.div(lane, cap), groups)
    lane_half = lax.div(lane, slots)
    scale = 1.0 / (ways * groups)

    def combine(k, h):
        at = slice(h * span, (h + 1) * span)
        part_send(k, h).wait_recv()
        acc[k - lowest(k), :, at] += part_in[k, :, at].astype(jnp.float32)

    def send_part(k, h):
        at = slice(h * span, (h + 1) * span)
        part_out[k, :, at] = acc[k, :, at].astype(jnp.bfloat16)
        part_send(k, h).start()

    def multiply(k):
        for i in range(experts):
            if k or i:
                row_wait(k, i).wait_recv()
            else:
                own_copy.wait()
        for h in range(parts):
            for n in range(span // tile):
                at = slice(h * span + n * tile, h * span + (n + 1) * tile)
                part = lax.dot_general(
                    cols[k], w[at, :], (((1,), (1,)), ((), ())),
                    preferred_element_type=jnp.float32,
                )
                if k % 2:
                    part_out[k, :, at] = part.astype(jnp.bfloat16)
                else:
                    acc[k, :, at] = part
            if k % 2:
                part_send(k, h).start()
            elif k:
                combine(k + 1, h)
                if lowest(k) == 2:
                    send_part(k, h)

    def add_squares(first):
        hid_arrive(first)
        hid_arrive(first + 1)
        flat = hidden[first : first + 2].reshape(2 * slots, units).astype(jnp.float32).T
        for h in range(2):
            for j in range(groups):
                keep = (lane_half == h) & (lane_j == j)
                turned[h * groups + j] = jnp.where(keep, flat, 0.0).astype(jnp.bfloat16)

        @pl.loop(0, width // chunk)
        def squares(n):
            at = pl.ds(pl.multiple_of(n * chunk, chunk), chunk)
            block = cols[first : first + 2, :, at].reshape(2 * slots, chunk)
            step = 128
            for m in range(units // step):
                rows = slice(m * step, (m + 1) * step)
                total_sq = None
                for b in range(2 * groups):
                    prod = jnp.dot(turned[b, rows, :], block, preferred_element_type=jnp.float32)
                    total_sq = prod * prod if total_sq is None else total_sq + prod * prod
                if first:
                    total_sq = total_sq + fisher_ref[rows, at]
                if first + 2 == ways:
                    total_sq = total_sq * scale
                fisher_ref[rows, at] = total_sq

    for k in order:
        multiply(k)
        if k == 0:
            add_squares(0)
    for first in range(2, ways, 2):
        add_squares(first)

    for h in range(parts):
        combine(1, h)
    bit = 2
    while bit < ways:
        for h in range(parts):
            for k in range(2 * bit, ways, 2 * bit):
                combine(k + bit, h)
                if lowest(k) == 2 * bit:
                    send_part(k, h)
            combine(bit, h)
        bit *= 2
    grad_ref[...] = acc[0].astype(jnp.bfloat16)
    for k in order:
        for i in range(experts):
            if k or i:
                row_send(k, i).wait_send()
        if k:
            hid_send(k).wait_send()
            for h in range(parts):
                part_send(k, h).wait_send()


def per_device(cotangent, expert_ids, gate_values, hidden, down_weight):
    experts = lax.axis_size("expert")
    ways = lax.axis_size("dp")
    groups, cap, units = hidden.shape[3], hidden.shape[4], hidden.shape[5]
    piece = groups * cap
    slots = experts * piece
    width = down_weight.shape[2]
    tokens, top = expert_ids.shape
    hbm_spec = pl.BlockSpec(memory_space=pltpu.HBM)
    vmem_spec = pl.BlockSpec(memory_space=pltpu.VMEM)
    bf16 = jnp.bfloat16
    operands = (
        expert_ids.T, gate_values.T, cotangent, hidden.reshape(slots, units), down_weight[0],
    )
    fisher, grad = pl.pallas_call(
        functools.partial(route_kernel, experts, ways, groups, cap),
        out_shape=(
            pltpu.VMEM((units, width), jnp.float32),
            pltpu.VMEM((slots, units), bf16),
        ),
        in_specs=[hbm_spec] * 5,
        out_specs=(vmem_spec, vmem_spec),
        scratch_shapes=[
            pltpu.VMEM((top, tokens), jnp.int32),
            pltpu.VMEM((top, tokens), jnp.float32),
            pltpu.VMEM((ways, tokens, width), bf16),
            pltpu.VMEM((units, width), bf16),
            pltpu.VMEM((ways, slots, width), bf16),
            pltpu.VMEM((ways, slots, width), bf16),
            pltpu.VMEM((ways, slots, units), bf16),
            pltpu.VMEM((ways, slots, units), bf16),
            pltpu.VMEM((ways, slots, units), bf16),
            pltpu.VMEM((ways, slots, units), jnp.float32),
            pltpu.VMEM((2 * groups, units, 2 * slots), bf16),
            pltpu.SemaphoreType.DMA((2,)),
            pltpu.SemaphoreType.DMA((ways,)),
            pltpu.SemaphoreType.DMA,
            pltpu.SemaphoreType.DMA,
            pltpu.SemaphoreType.DMA,
            pltpu.SemaphoreType.DMA((ways, experts)),
            pltpu.SemaphoreType.DMA((ways, experts)),
            pltpu.SemaphoreType.DMA((ways,)),
            pltpu.SemaphoreType.DMA((ways,)),
            pltpu.SemaphoreType.DMA((ways, 2)),
            pltpu.SemaphoreType.DMA((ways, 2)),
        ],
        compiler_params=pltpu.CompilerParams(
            collective_id=0, has_side_effects=True, vmem_limit_bytes=50 * 2**20
        ),
        name="route",
    )(*(pltpu.with_memory_space_constraint(x, pltpu.HBM) for x in operands))
    return (fisher[None], grad.reshape(hidden.shape))


def solution(mesh):
    in_specs = (
        P(("group", "expert", "dp"), None),
        P(("group", "expert", "dp"), None),
        P(("group", "expert", "dp"), None),
        P(("group", "expert"), "dp", None, None, None, None),
        P("expert", None, "dp"),
    )
    out_specs = (
        P(("group", "expert"), None, "dp"),
        P(("group", "expert"), "dp", None, None, None, None),
    )
    return jax.shard_map(
        per_device, mesh=mesh, in_specs=in_specs, out_specs=out_specs, check_vma=False
    )
```
